512 devices in a mesh: req: 128 (over z, y_lo, x), tp: 4 (over y_hi, core).
Axes of the slice: x: 4, y: 4 (y_hi: 2, y_lo: 2; y = y_hi * 2 + y_lo), z: 16, core: 2. Of those that a mesh axis runs over, the one named last changes fastest.
Arguments:
- hidden: bfloat16 [8192, 2048], P('req'), may hold values from -6 to 6
- draft_query: bfloat16 [8192, 2048], P('req', 'tp'), may hold values from -180 to 180
- draft_kv: bfloat16 [2, 8192, 2048], P(None, 'req', 'tp'), may hold values from -6 to 6
- cache_kv: bfloat16 [2, 32768, 2048], P(None, 'req', 'tp'), may hold values from -6 to 6
- piece_offset: int32 [256], P('req'), may hold values from 0 to 3
- piece_length: int32 [256], P('req'), may hold values from 1 to 128
- ancestors: int32 [8192, 64], P('req'), may hold values from 0 to 1, as said below
- out_proj: bfloat16 [2048, 2048], P('tp'), may hold values from -0.125 to 0.125
- ffn_gain: float32 [2048], replicated, may hold values from 0.1 to 1.9
- router_w: bfloat16 [2048, 64], replicated, may hold values from -0.125 to 0.125
- expert_gate_up: bfloat16 [2, 2048, 65536], P(None, None, ('req', 'tp')), may hold values from -0.125 to 0.125
- expert_down: bfloat16 [65536, 2048], P(('req', 'tp')), may hold values from -1.5 to 1.5
- expert_ids: int32 [8192, 8], P('req'), may hold values from 0 to 63, all different within a row; in each aligned block of 64 rows (0 to 63, 64 to 127, ...) at most 12 rows name the same one
- accepted_ids: int32 [1024], P('req'), may hold values from 0 to 63
Outputs:
- layer_out: bfloat16 [8192, 2048], P('req', 'tp')
- attended: bfloat16 [8192, 2048], P('req', 'tp')
- accepted_kv: bfloat16 [2, 1024, 2048], P(None, 'req', 'tp')
The draws below stay inside these ranges and needn't reach their ends.
Inputs may be any that keep to these rules, and one draw needn't show every extreme that they name: Piece p of device d belongs to the request of device (d - piece_offset[p]) mod 128. Within each request's 64 rows, row i marks node i and all its ancestors; node 0 is the root and every other node's parent has a lower number. `expert_ids`: each row names 8 different experts; in the rows of one device no expert is named by more than 12 rows, a bound that some block reaches.
All inputs are finite; a program needn't handle non-finite values.
Results may differ from the reference program's by a relative error of at most 0.03.
Values may be sent and summed in bfloat16 or wider, within the bound.
A program may use at most 64 MiB of HBM per device.

```python
import math
import jax
import jax.numpy as jnp
import numpy as np
from jax import lax

D = 2048
H = 16
HD = 128
FF_E = 1024
DRAFT = 64
PIECES = 2
PIECE = 128
SPAN = 4
ACC = 8
EXPERTS = 64
TOP = 8
CAP = 12
TOKENS = 8192
N_REQ = 128
N_TP = 4


def draw_draft_query(key, part):
    base = 3.0 * jnp.clip(jax.random.normal(key, (TOKENS, H * HD), jnp.float32), -6.0, 6.0)
    return base.astype(jnp.bfloat16)


def draw_ancestors(key, part):
    requests = TOKENS // DRAFT
    raw = jax.random.randint(key, (requests, DRAFT), 0, 1 << 20)
    node = jnp.arange(DRAFT, dtype=jnp.int32)
    parent = raw % jnp.maximum(node, 1)[None, :]
    links = ((node[None, :, None] == node[None, None, :]) | (parent[:, :, None] == node[None, None, :])).astype(jnp.int32)
    for step in range(8):
        links = (jnp.einsum('rij,rjk->rik', links, links) > 0).astype(jnp.int32)
    return links.reshape(TOKENS, DRAFT)


def set_ends(values, rng, least, high):
    longest = values.shape.index(max(values.shape))
    spots = []
    for shift in (0, 1):
        where = [jax.random.randint(jax.random.fold_in(rng, axis), (), 0, length) for axis, length in enumerate(values.shape)]
        where[longest] = (where[longest] + shift) % values.shape[longest]
        spots.append(tuple(where))
    return values.at[spots[0]].set(least).at[spots[1]].set(high)


def levels(key, shape, split, least, largest):
    loudness = 1.0
    for dim, blocks in split:
        steps = jax.random.uniform(jax.random.fold_in(jax.random.fold_in(key, 6), dim), (blocks,), jnp.float32, least / len(split), largest / len(split))
        loudness = loudness * jnp.repeat(jnp.exp(steps), shape[dim] // blocks).reshape((-1,) + (1,) * (len(shape) - 1 - dim))
    return loudness


def assign_block(own_key, own, number, rows, number_of, top, most, slope):
    order = jax.random.permutation(own_key, number_of)
    heavy_load, usual = load_shares(number_of, rows * top, most, slope, True), load_shares(number_of, rows * top, most, slope, False)
    places = jnp.arange(number_of)

    def named(sizes, offset_by):
        used = int((sizes > 0).sum())
        fixed = max(1, used // 4)
        moved = fixed + (places - fixed + offset_by * (used - fixed)) % max(1, number_of - fixed)
        return jnp.zeros((number_of,), jnp.int32).at[order[jnp.where(places < fixed, places, moved)]].set(jnp.asarray(sizes, jnp.int32))

    sizes = jnp.where(number % 4 == 0, named(heavy_load, number // 4), named(usual, number - number // 4 - 1))
    mixed = jax.random.permutation(jax.random.fold_in(own, 3), number_of)
    giver, receiver = mixed[0:number_of // 2 * 2:2], mixed[1:number_of // 2 * 2:2]
    slack = jnp.minimum(sizes[giver] - 1, most - sizes[receiver]) // 2
    slack = jnp.where((giver == order[0]) | (receiver == order[0]) | (sizes[receiver] == 0), 0, jnp.maximum(slack, 0))
    moved = jax.random.randint(jax.random.fold_in(own, 4), (number_of // 2,), 0, 1 << 20) % (slack + 1)
    sizes = sizes.at[giver].add(-moved).at[receiver].add(moved)
    members = jnp.searchsorted(jnp.cumsum(sizes), jnp.arange(rows * top), side="right").astype(jnp.int32)
    table = members.reshape(top, rows).T
    table = table[jax.random.permutation(jax.random.fold_in(own, 1), rows)]
    offset_by = jax.random.randint(jax.random.fold_in(own, 2), (rows, 1), 0, top)
    return jnp.take_along_axis(table, (jnp.arange(top)[None, :] + offset_by) % top, axis=1)


def load_shares(amount, total, bound, lean, full):
    loads = [(1 << 20) // math.isqrt(rank ** lean) + 1 for rank in range(1, amount + 1)]
    largest = bound if full else min(bound, max(-(-total // amount), total * loads[0] // sum(loads)))
    least = 1 if total - largest >= amount - 1 else 0
    given, rest = [largest] + [least] * (amount - 1), total - largest - least * (amount - 1)
    while rest > 0:
        free = [i for i in range(1, amount) if given[i] < largest] or [i for i in range(1, amount) if given[i] < bound]
        mass, left = sum([loads[i] for i in free]), rest
        for i in free:
            more = min(bound - given[i], max(1, left * loads[i] // mass), rest)
            given[i] = given[i] + more
            rest = rest - more
    return np.array(given)


def normal_values(rng, shape, scale, most, shards=(), kind=jnp.bfloat16):
    values = scale * jax.random.normal(rng, shape, jnp.float32)
    if shards:
        values = values * levels(rng, shape, shards, -0.22, 0.18)
    return jnp.clip(values, -most, most).astype(kind)


def setup_inputs(seed: int = 0) -> dict:
    streams_of = jax.random.split(jax.random.key(seed), 15)
    hidden = normal_values(streams_of[0], (TOKENS, D), 1.0, 6.0, ((0, 128),))
    draft_query = draw_draft_query(jax.random.fold_in(streams_of[14], 71), 0)
    draft_kv = normal_values(streams_of[2], (2, TOKENS, H * HD), 1.0, 6.0, ((1, 128), (2, 4)))
    cache_kv = normal_values(streams_of[3], (2, N_REQ * PIECES * PIECE, H * HD), 1.0, 6.0, ((1, 128), (2, 4)))
    piece_offset = set_ends(jax.random.randint(streams_of[4], (N_REQ * PIECES,), 0, SPAN), jax.random.fold_in(streams_of[4], 1), 0, SPAN - 1).astype(jnp.int32)
    piece_length = set_ends(jax.random.randint(streams_of[5], (N_REQ * PIECES,), 1, PIECE + 1), jax.random.fold_in(streams_of[5], 1), 1, PIECE).astype(jnp.int32)
    ancestors = draw_ancestors(jax.random.fold_in(streams_of[14], 71), 0)
    out_proj = normal_values(streams_of[7], (H * HD, D), (H * HD) ** -0.5, 0.125, ((0, 4),))
    ffn_gain = jnp.clip(1.0 + 0.18 * jax.random.normal(streams_of[8], (D,), jnp.float32), 0.1, 1.9)
    router_w = normal_values(streams_of[9], (D, EXPERTS), D ** -0.5, 0.125)
    expert_gate_up = normal_values(streams_of[10], (2, D, EXPERTS * FF_E), D ** -0.5, 0.125, ((2, 512),))
    expert_down = normal_values(streams_of[11], (EXPERTS * FF_E, D), (FF_E // 64) ** -0.5, 1.5, ((0, 512),))
    expert_ids_keys = jax.random.split(jax.random.fold_in(streams_of[12], 1), TOKENS // DRAFT)
    expert_ids_turns = jax.random.permutation(jax.random.fold_in(streams_of[12], 3), TOKENS // DRAFT)
    expert_ids = jax.vmap(lambda own, number: assign_block(jax.random.fold_in(streams_of[12], 2), own, number, DRAFT, EXPERTS, TOP, CAP, 2))(expert_ids_keys, expert_ids_turns).reshape((TOKENS, TOP))
    accepted_ids = set_ends(jax.random.randint(streams_of[13], (N_REQ * ACC,), 0, DRAFT), jax.random.fold_in(streams_of[13], 1), 0, DRAFT - 1).astype(jnp.int32)
    return dict(hidden=hidden, draft_query=draft_query, draft_kv=draft_kv, cache_kv=cache_kv, piece_offset=piece_offset, piece_length=piece_length, ancestors=ancestors, out_proj=out_proj, ffn_gain=ffn_gain, router_w=router_w, expert_gate_up=expert_gate_up, expert_down=expert_down, expert_ids=expert_ids, accepted_ids=accepted_ids)


NEG = -1e+30

def partials(scores, mask, values, equation):
    top = lax.optimization_barrier(jnp.max(jnp.where(mask, scores, NEG), axis=-1))
    weights = jnp.where(mask, jnp.exp(scores - top[..., None]), 0.0)
    total = lax.optimization_barrier(jnp.sum(weights, axis=-1))
    rounded = lax.optimization_barrier(weights.astype(jnp.bfloat16))
    acc = jnp.einsum(equation, rounded.astype(jnp.float32), values)
    return (top, total, acc)

def reference(hidden, draft_query, draft_kv, cache_kv, piece_offset, piece_length, ancestors, out_proj, ffn_gain, router_w, expert_gate_up, expert_down, expert_ids, accepted_ids):
    scale = HD ** (-0.5)
    query = draft_query.reshape(N_REQ, DRAFT, H, HD)
    draft_pair = draft_kv.reshape(2, N_REQ, DRAFT, H, HD)
    cache_pair = cache_kv.reshape(2, N_REQ, PIECES, PIECE, H, HD)
    offsets = piece_offset.reshape(N_REQ, PIECES)
    lengths = piece_length.reshape(N_REQ, PIECES)
    tree = ancestors.reshape(N_REQ, DRAFT, DRAFT)
    slots = jnp.arange(PIECE, dtype=jnp.int32)
    reach = jnp.arange(SPAN, dtype=jnp.int32)

    def one_request(req):
        devices = ((req + reach) % N_REQ).astype(jnp.int32)
        qf = query[req].astype(jnp.float32)
        keys = jnp.take(cache_pair[0], devices, axis=0).astype(jnp.float32)
        values = jnp.take(cache_pair[1], devices, axis=0).astype(jnp.float32)
        valid = (jnp.take(offsets, devices, axis=0) == reach[:, None])[:, :, None] & (slots[None, None, :] < jnp.take(lengths, devices, axis=0)[:, :, None])
        scores = jnp.einsum('thd,kpshd->kpths', qf, keys) * scale
        top, total, acc = partials(scores, valid[:, :, None, None, :], values, 'kpths,kpshd->kpthd')
        own_keys = draft_pair[0, req].astype(jnp.float32)
        own_values = draft_pair[1, req].astype(jnp.float32)
        dscores = jnp.einsum('thd,shd->ths', qf, own_keys) * scale
        dtop, dtotal, dacc = partials(dscores, (tree[req] > 0)[:, None, :], own_values, 'ths,shd->thd')
        tops = jnp.concatenate([top.reshape(-1, DRAFT, H), dtop[None]])
        totals = jnp.concatenate([total.reshape(-1, DRAFT, H), dtotal[None]])
        accs = jnp.concatenate([acc.reshape(-1, DRAFT, H, HD), dacc[None]])
        best = lax.optimization_barrier(jnp.max(tops, axis=0))
        factor = jnp.exp(tops - best[None])
        out = lax.optimization_barrier(jnp.sum(factor[..., None] * accs, axis=0)) / lax.optimization_barrier(jnp.sum(factor * totals, axis=0))[..., None]
        return out.astype(jnp.bfloat16).reshape(DRAFT, H * HD)
    attended = lax.map(one_request, jnp.arange(N_REQ, dtype=jnp.int32)).reshape(TOKENS, H * HD)
    attn_proj = jnp.dot(attended, out_proj, preferred_element_type=jnp.float32)
    residual = (hidden.astype(jnp.float32) + attn_proj).astype(jnp.bfloat16)
    resf = residual.astype(jnp.float32)
    normed = (resf * lax.rsqrt(lax.optimization_barrier(jnp.mean(resf * resf, axis=1, keepdims=True)) + 1e-06) * ffn_gain).astype(jnp.bfloat16)
    logits = jnp.dot(normed, router_w, preferred_element_type=jnp.float32)
    chosen = jnp.take_along_axis(logits, expert_ids, axis=1)
    gates = jax.nn.softmax(chosen, axis=1).astype(jnp.bfloat16)
    routed = lax.optimization_barrier(jnp.sum((expert_ids[:, :, None] == jnp.arange(EXPERTS, dtype=jnp.int32)).astype(jnp.int32), axis=1))
    blocks = routed.reshape(N_REQ, DRAFT, EXPERTS)
    rank = (jnp.cumsum(blocks, axis=1) - blocks).reshape(TOKENS, EXPERTS)
    slot_of = jnp.take_along_axis(rank, expert_ids, axis=1)
    device = (jnp.arange(TOKENS, dtype=jnp.int32) // DRAFT)[:, None]
    flat_pos = ((expert_ids * N_REQ + device) * CAP + slot_of).reshape(-1).astype(jnp.int32)
    row_ids = jnp.broadcast_to(jnp.arange(TOKENS, dtype=jnp.int32)[:, None], (TOKENS, TOP)).reshape(-1)
    table = jnp.full((EXPERTS * N_REQ * CAP,), TOKENS, jnp.int32).at[flat_pos].set(row_ids).reshape(EXPERTS, N_REQ * CAP)
    gate_table = jnp.zeros((EXPERTS * N_REQ * CAP,), jnp.float32).at[flat_pos].set(gates.astype(jnp.float32).reshape(-1)).reshape(EXPERTS, N_REQ * CAP)
    padded = jnp.concatenate([normed, jnp.zeros((1, D), jnp.bfloat16)])
    groups = 2 * N_TP
    width = FF_E // groups

    def one_expert(carry, expert):
        rows = table[expert]
        inputs = jnp.take(padded, rows, axis=0)
        pair = lax.dynamic_slice_in_dim(expert_gate_up, expert * FF_E, FF_E, 2)
        gate = jnp.dot(inputs, pair[0], preferred_element_type=jnp.float32)
        upper = jnp.dot(inputs, pair[1], preferred_element_type=jnp.float32)
        act = (jax.nn.silu(gate) * upper).astype(jnp.bfloat16)
        down = lax.dynamic_slice_in_dim(expert_down, expert * FF_E, FF_E, 0)
        part = jnp.einsum('rgf,gfm->rgm', act.reshape(-1, groups, width).astype(jnp.float32), down.reshape(groups, width, D).astype(jnp.float32)).astype(jnp.bfloat16)
        summed = lax.optimization_barrier(jnp.sum(part.astype(jnp.float32), axis=1)) * gate_table[expert][:, None]
        return (carry.at[rows].add(summed, mode='drop'), None)
    moe, _ = lax.scan(one_expert, jnp.zeros((TOKENS, D), jnp.float32), jnp.arange(EXPERTS, dtype=jnp.int32))
    layer_out = (resf + moe).astype(jnp.bfloat16)
    base = jnp.arange(N_REQ * ACC, dtype=jnp.int32) // ACC * DRAFT
    accepted_kv = jnp.take(draft_kv, (accepted_ids + base).astype(jnp.int32), axis=1)
    return (layer_out, attended, accepted_kv)
```

```python
import functools

import jax
import jax.numpy as jnp
from jax import lax
from jax.experimental import pallas as pl
from jax.experimental.pallas import tpu as pltpu
from jax.sharding import PartitionSpec as P

HD = 128
HEADS = 4
PIECES = 2
PIECE = 128
SPAN = 4
T = 64
C = 512
D = 2048
CAP = 12
Z = 16
N_REQ = 128
NEG = -1e30
NONE = -100.0
F32 = jnp.float32
BF16 = jnp.bfloat16
MESH = pl.DeviceIdType.MESH

ORDER = [0, 1, -1, 2, -2, 3, -3, 4, -4, 5, -5, 6, -6, 7, -7, 8]
POS = {rel: at for at, rel in enumerate(ORDER)}
FLIPS = [(a, b, h) for h in (0, 1) for a in (0, 1) for b in (0, 1)]


def iota(shape, dim):
    return lax.broadcasted_iota(jnp.int32, shape, dim)


def nt(a, b):
    return lax.dot_general(a, b, (((1,), (1,)), ((), ())), preferred_element_type=F32)


def tn(a, b):
    return lax.dot_general(a, b, (((0,), (0,)), ((), ())), preferred_element_type=F32)


def nn(a, b):
    return jnp.dot(a, b, preferred_element_type=F32)


def softmax_part(scores, mask, values):
    top = jnp.max(jnp.where(mask, scores, NEG), axis=1, keepdims=True)
    weights = jnp.where(mask, jnp.exp(scores - top), 0.0)
    total = jnp.sum(weights, axis=1, keepdims=True)
    return top, total, nn(weights.astype(BF16), values)


def kernel(
    q_ref, dkv_ref, ckv_ref, off_ref, len_ref, anc_ref, hid_ref, op_ref, gain_ref, rw_ref,
    gu_ref, dn_ref, ids_ref, accid_ref,
    out_ref, att_ref, acc_ref,
    w_all, d_all, q_in, part_out, stat_out, part_in, stat_in, proj_out, proj_in,
    code_out, code_in, gate_out, gate_in, rows, full, hot, packed, x_in, normed, act, o_out, t_in,
    moe, rs_out, rs_in,
    wl_sem, ws_sem, wr_sem, qs_sem, qr_sem, ps_sem, pr_sem, as_sem, ar_sem, fs_sem, fr_sem,
    cs_sem, cr_sem, gs_sem, gr_sem, zs_sem, zr_sem, ds_sem, dr_sem, ts_sem, tr_sem, ss_sem, sr_sem,
):
    req, tp = lax.axis_index("req"), lax.axis_index("tp")
    z, yl, x = req // 8, (req // 4) % 2, req % 4
    xh, xl = x // 2, x % 2
    yh, c = tp // 2, tp % 2
    scale = HD ** (-0.5)
    sends = []

    def along(k):
        return (lax.rem(req + (k + N_REQ), N_REQ), tp)

    def plane(d):
        return (lax.rem(z + (d + Z), Z) * 8 + yl * 4 + x, tp)

    def flipped(a, b, h, core):
        y2 = 1 - yl if a else yl
        x2 = 3 - x if b else x
        h2 = 1 - yh if h else yh
        return (z * 8 + y2 * 4 + x2, h2 * 2 + core)

    x_partner = (req + 1 - 2 * xl, tp)
    core_partner = (req, yh * 2 + 1 - c)

    def copy(src, dst, send, recv, to):
        return pltpu.make_async_remote_copy(
            src_ref=src, dst_ref=dst, send_sem=send, recv_sem=recv, device_id=to, device_id_type=MESH
        )

    def send(src, dst, send_sem, recv_sem, to):
        one = copy(src, dst, send_sem, recv_sem, to)
        one.start()
        sends.append(one)

    def arrived(dst, send_sem, recv_sem):
        copy(dst, dst, send_sem, recv_sem, core_partner).wait_recv()

    ids = ids_ref[...].astype(F32).astype(BF16)
    eye = (iota((16, 8), 0) == iota((16, 8), 1)).astype(F32).astype(BF16)
    ids_t = nt(eye, ids)
    n_row = iota((128, T), 0)
    j_row = n_row & 7
    e_row = (n_row >> 3) * 4 + ((yl + (j_row >> 1)) & 1) * 2 + ((xh + j_row) & 1)
    e_row = jnp.where(j_row < 4, e_row, -1)
    e_rowf = e_row.astype(F32)
    routed_t = jnp.zeros((128, T), F32)
    for j in range(8):
        routed_t += (ids_t[j : j + 1, :] == e_rowf).astype(F32)
    routed_t = routed_t.astype(BF16)
    place = []
    for par in (0, 1):
        lane = iota((T, 128), 1) - T * par
        t_row = iota((T, 128), 0)
        later = ((lane > t_row) & (lane < T)).astype(F32).astype(BF16)
        same = (lane == t_row).astype(F32).astype(BF16)
        place.append(same)
        rank = nn(routed_t, later)
        there = nn(routed_t, same)
        code_out[par] = jnp.where(there > 0.5, rank, NONE).reshape(Z, 8, 128)

    barrier = pltpu.get_barrier_semaphore()
    peers = [along(k) for k in (1, 2, 3, -1, -2, -3)]
    peers += [plane(d) for d in range(-8, 8) if d]
    peers += [flipped(a, b, h, 1 - c) for a, b, h in FLIPS]
    peers += [flipped(a, b, h, c) for a, b, h in FLIPS if a or b or h]
    peers += [x_partner]
    for peer in peers:
        pl.semaphore_signal(barrier, inc=1, device_id=peer, device_id_type=MESH)
    pl.semaphore_wait(barrier, len(peers))

    for k in (1, 2, 3):
        send(q_ref, q_in.at[k], qs_sem.at[k], qr_sem.at[k], along(k))
    for d in range(-8, 8):
        if d:
            at = POS[-d]
            to_z = lax.rem(z + (d + Z), Z)
            send(code_out.at[at % 2, to_z], code_in.at[at], cs_sem.at[at], cr_sem.at[at], plane(d))
    code_in[0] = code_out[0, z]
    q_in[0] = q_ref[...]

    local = [
        pltpu.make_async_copy(gu_ref.at[0], w_all.at[0, :, 0:128], wl_sem.at[0]),
        pltpu.make_async_copy(gu_ref.at[1], w_all.at[0, :, 128:256], wl_sem.at[1]),
        pltpu.make_async_copy(dn_ref, d_all.at[0:128], wl_sem.at[2]),
    ]
    for one in local:
        one.start()
    for slot, to in ((1, core_partner), (2, x_partner)):
        for i in (0, 1):
            send(gu_ref.at[i], w_all.at[slot, :, i * 128 : i * 128 + 128],
                 ws_sem.at[slot, i], wr_sem.at[slot, i], to)
        send(dn_ref, d_all.at[slot * 128 : slot * 128 + 128], ws_sem.at[slot, 2], wr_sem.at[slot, 2], to)

    tree = anc_ref[...] > 0
    draft = []
    for h in range(HEADS):
        cols = slice(h * HD, h * HD + HD)
        scores = nt(q_ref[:, cols], dkv_ref[0, :, cols]) * scale
        draft.append(softmax_part(scores, tree, dkv_ref[1, :, cols]))

    pick = jnp.zeros((16, 128), jnp.int32)
    a_row = iota((16, 128), 0)
    for i in range(8):
        pick = jnp.where((a_row & 7) == i, accid_ref[i], pick)
    pick = pick + T * (a_row >> 3)
    chosen = (iota((16, 128), 1) == pick).astype(F32).astype(BF16)
    acc_ref[...] = nn(chosen, dkv_ref[...].reshape(128, C)).astype(BF16)

    for k in (1, 2, 3):
        arrived(q_in.at[k], qs_sem.at[k], qr_sem.at[k])
    parts = []
    for p in range(PIECES):
        query = q_in[off_ref[p]]
        valid = iota((T, PIECE), 1) < len_ref[p]
        mine = []
        for h in range(HEADS):
            cols = slice(h * HD, h * HD + HD)
            slots = slice(p * PIECE, p * PIECE + PIECE)
            scores = nt(query[:, cols], ckv_ref[0, slots, cols]) * scale
            mine.append(softmax_part(scores, valid, ckv_ref[1, slots, cols]))
        parts.append(mine)
    lanes = iota((T, 128), 1)
    own = []
    for k in (1, 2, 3, 0):
        stats = jnp.zeros((T, 128), F32)
        for h in range(HEADS):
            tops = [jnp.where(off_ref[p] == k, parts[p][h][0], NEG) for p in range(PIECES)]
            top = jnp.maximum(tops[0], tops[1])
            total, acc = 0.0, 0.0
            for p in range(PIECES):
                factor = jnp.where(off_ref[p] == k, jnp.exp(tops[p] - top), 0.0)
                total = total + factor * parts[p][h][1]
                acc = acc + factor * parts[p][h][2]
            if k == 0:
                own.append((top, total, acc))
                continue
            part_out[k, :, h * HD : h * HD + HD] = acc.astype(BF16)
            stats = jnp.where(lanes == h, top, stats)
            stats = jnp.where(lanes == 4 + h, total, stats)
        if k:
            stat_out[k] = stats
            send(part_out.at[k], part_in.at[k], ps_sem.at[0, k], pr_sem.at[0, k], along(-k))
            send(stat_out.at[k], stat_in.at[k], ps_sem.at[1, k], pr_sem.at[1, k], along(-k))

    for k in (1, 2, 3):
        arrived(part_in.at[k], ps_sem.at[0, k], pr_sem.at[0, k])
        arrived(stat_in.at[k], ps_sem.at[1, k], pr_sem.at[1, k])
    for h in range(HEADS):
        cols = slice(h * HD, h * HD + HD)
        every = [draft[h], own[h]]
        for k in (1, 2, 3):
            stats = stat_in[k]
            every.append((stats[:, h : h + 1], stats[:, 4 + h : 5 + h], part_in[k, :, cols].astype(F32)))
        best = every[0][0]
        for top, _, _ in every[1:]:
            best = jnp.maximum(best, top)
        total, acc = 0.0, 0.0
        for top, one_total, one_acc in every:
            factor = jnp.exp(top - best)
            total = total + factor * one_total
            acc = acc + factor * one_acc
        att_ref[:, cols] = (acc / total).astype(BF16)

    attended = att_ref[...]
    for q in range(4):
        proj_out[q] = nn(attended, op_ref[:, q * C : q * C + C])
    others = [(1, 1), (1, 0), (0, 1)]
    for i, (h, k) in enumerate(others):
        core = 1 - c if k else c
        tp2 = (1 - yh if h else yh) * 2 + core
        part_out[4 + i] = proj_out[tp2].astype(BF16)
        send(part_out.at[4 + i], proj_in.at[i], as_sem.at[i], ar_sem.at[i], (req, tp2))
    cols = pl.ds(pl.multiple_of(tp * C, C), C)
    total = hid_ref[:, cols].astype(F32) + proj_out[tp]
    for i in range(3):
        arrived(proj_in.at[i], as_sem.at[i], ar_sem.at[i])
        total = total + proj_in[i].astype(F32)
    residual = total.astype(BF16)
    rows[0] = residual

    def pass_on(rel):
        step = 1 if rel <= 0 else -1
        new = rel - step
        send(rows.at[POS[rel]], rows.at[POS[new]], zs_sem.at[POS[new]], zr_sem.at[POS[new]], plane(step))

    def rows_arrived(rel):
        arrived(rows.at[POS[rel]], zs_sem.at[POS[rel]], zr_sem.at[POS[rel]])

    pass_on(0)
    send(rows.at[0], rows.at[POS[1]], zs_sem.at[POS[1]], zr_sem.at[POS[1]], plane(-1))
    full[tp] = residual
    for i, (h, k) in enumerate(others):
        core = 1 - c if k else c
        tp2 = (1 - yh if h else yh) * 2 + core
        send(rows.at[0], full.at[tp], fs_sem.at[i], fr_sem.at[i], (req, tp2))

    for d in range(-8, 8):
        if d:
            at = POS[-d]
            arrived(code_in.at[at], cs_sem.at[at], cr_sem.at[at])

    def hot_group(n):
        for j in range(4):
            for pair in (0, 1):
                at = 4 * n + 2 * pair
                line = jnp.maximum(
                    code_in[at, j : j + 1, :] + CAP * 2.0 * pair,
                    code_in[at + 1, j : j + 1, :] + CAP * (2.0 * pair + 1.0),
                )
                match = iota((48, 128), 0).astype(F32) == line
                hot[n, j * 48 : j * 48 + 48, pair * 128 : pair * 128 + 128] = match.astype(F32).astype(BF16)

    for n in range(4):
        hot_group(n)

    def gates():
        for i, (h, k) in enumerate(others):
            core = 1 - c if k else c
            tp2 = (1 - yh if h else yh) * 2 + core
            arrived(full.at[tp2], fs_sem.at[i], fr_sem.at[i])
        square = jnp.zeros((T, 1), F32)
        for q in range(4):
            part = full[q].astype(F32)
            square = square + jnp.sum(part * part, axis=1, keepdims=True)
        inverse = lax.rsqrt(square * (1.0 / D) + 1e-06)
        logits = jnp.zeros((T, 64), F32)
        for q in range(4):
            some = (full[q].astype(F32) * inverse * gain_ref[:, q * C : q * C + C]).astype(BF16)
            logits = logits + nn(some, rw_ref[q * C : q * C + C, :])
        named = jnp.zeros((T, 64), F32)
        ids_i = ids_ref[...]
        for j in range(8):
            named = named + (ids_i[:, j : j + 1] == iota((T, 64), 1)).astype(F32)
        top = jnp.max(jnp.where(named > 0.5, logits, NEG), axis=1, keepdims=True)
        weight = jnp.where(named > 0.5, jnp.exp(logits - top), 0.0)
        gate = (weight / jnp.sum(weight, axis=1, keepdims=True)).astype(BF16)
        n2 = iota((128, 64), 0)
        j2 = n2 & 7
        e2 = (n2 >> 3) * 4 + ((yl + (j2 >> 1)) & 1) * 2 + ((xh + j2) & 1)
        select = ((j2 < 4) & (e2 == iota((128, 64), 1))).astype(F32).astype(BF16)
        gate_t = nt(select, gate).astype(BF16)
        for par in (0, 1):
            gate_out[par] = nn(gate_t, place[par]).reshape(Z, 8, 128)
        for d in range(-8, 8):
            if d:
                at = POS[-d]
                to_z = lax.rem(z + (d + Z), Z)
                send(gate_out.at[at % 2, to_z], gate_in.at[at], gs_sem.at[at], gr_sem.at[at], plane(d))
        gate_in[0] = gate_out[0, z]

    def x_cols(core, h=None):
        tp2 = yh * 2 + core if h is None else (1 - yh if h else yh) * 2 + core
        return pl.ds(pl.multiple_of(tp2 * C, C), C)

    special = []

    def dispatch(n):
        packed[n] = nn(hot[n], rows[4 * n : 4 * n + 4].reshape(256, C)).astype(BF16)
        m, core = n // 2, n % 2
        for i, (a, b, h) in enumerate(FLIPS):
            j = a * 2 + b
            src = packed.at[n, j * 48 : j * 48 + 48]
            dst = x_in.at[m, j * 48 : j * 48 + 48, x_cols(c)]
            if i:
                send(src, dst, ds_sem.at[n, i], dr_sem.at[m, i, c], flipped(a, b, h, core))
                continue

            @pl.when(c == core)
            def _():
                dst[...] = src[...]

            one = copy(src, dst, ds_sem.at[n, i], dr_sem.at[m, i, c], (req, yh * 2 + 1 - c))

            @pl.when(c != core)
            def _():
                one.start()

            special.append((core, one))

    for s in range(1, 9):
        if s < 8:
            rows_arrived(-s)
            if s < 7:
                pass_on(-s)
        rows_arrived(s)
        if s < 8:
            pass_on(s)
        if s % 2 == 0:
            dispatch(s // 2 - 1)
        if s == 3:
            gates()
        if s == 7:
            for i in (0, 1):
                arrived(w_all.at[2, :, i * 128 : i * 128 + 128], ws_sem.at[2, i], wr_sem.at[2, i])
            arrived(d_all.at[256:384], ws_sem.at[2, 2], wr_sem.at[2, 2])
            send(w_all.at[2], w_all.at[3], ws_sem.at[3, 0], wr_sem.at[3, 0], core_partner)
            send(d_all.at[256:384], d_all.at[384:512], ws_sem.at[3, 1], wr_sem.at[3, 1], core_partner)

    for one in local:
        one.wait()
    for i in (0, 1):
        arrived(w_all.at[1, :, i * 128 : i * 128 + 128], ws_sem.at[1, i], wr_sem.at[1, i])
    arrived(d_all.at[128:256], ws_sem.at[1, 2], wr_sem.at[1, 2])
    arrived(w_all.at[3], ws_sem.at[3, 0], wr_sem.at[3, 0])
    arrived(d_all.at[384:512], ws_sem.at[3, 1], wr_sem.at[3, 1])

    for m in (0, 1):
        for i, (a, b, h) in enumerate(FLIPS):
            j = a * 2 + b
            for k in (0, 1):
                if i or k:
                    core = 1 - c if k else c
                    arrived(x_in.at[m, j * 48 : j * 48 + 48, x_cols(core, h)],
                            ds_sem.at[0, i], dr_sem.at[m, i, core])

        @pl.loop(0, 4)
        def _(j):
            some = pl.ds(pl.multiple_of(j * 48, 16), 48)
            block = x_in[m, some, :].astype(F32)
            mean = jnp.sum(block * block, axis=1, keepdims=True) * (1.0 / D)
            normed[some, :] = (block * lax.rsqrt(mean + 1e-06) * gain_ref[...]).astype(BF16)

        @pl.loop(0, 4)
        def _(j):
            both = nn(normed[...], w_all[j])
            gate, upper = both[:, :128], both[:, 128:]
            hidden = gate / (1.0 + jnp.exp(-gate)) * upper
            act[:, pl.ds(pl.multiple_of(j * 128, 128), 128)] = hidden.astype(BF16)

        @pl.loop(0, 4)
        def _(q):
            some = pl.ds(pl.multiple_of(q * C, C), C)
            o_out[m, :, some] = nn(act[...], d_all[:, some]).astype(BF16)

        for i, (a, b, h) in enumerate(FLIPS):
            j = a * 2 + b
            for k in (0, 1):
                core = 1 - c if k else c
                src = o_out.at[m, j * 48 : j * 48 + 48, x_cols(core, h)]
                dst = t_in.at[2 * m + c, h, j * 48 : j * 48 + 48]
                if i or k:
                    send(src, dst, ts_sem.at[m, i, k], tr_sem.at[2 * m + c, i], flipped(a, b, h, core))
                else:
                    dst[...] = src[...]

    for d in range(-8, 8):
        if d:
            at = POS[-d]
            arrived(gate_in.at[at], gs_sem.at[at], gr_sem.at[at])

    def combine(n):
        for i, (a, b, h) in enumerate(FLIPS):
            j = a * 2 + b

            def wait(i=i, h=h, j=j):
                arrived(t_in.at[n, h, j * 48 : j * 48 + 48], ts_sem.at[0, i, 0], tr_sem.at[n, i])

            if i:
                wait()
            else:
                pl.when(c != n % 2)(wait)
        blocks = []
        for j in range(4):
            halves = []
            for pair in (0, 1):
                at = 4 * n + 2 * pair
                gate = gate_in[at, j : j + 1, :] + gate_in[at + 1, j : j + 1, :]
                some = hot[n, j * 48 : j * 48 + 48, pair * 128 : pair * 128 + 128].astype(F32)
                halves.append(some * gate)
            blocks.append(jnp.concatenate(halves, axis=1))
        weight = jnp.concatenate(blocks, axis=0).astype(BF16)
        result = tn(weight, t_in[n, 0]) + tn(weight, t_in[n, 1])
        moe[4 * n : 4 * n + 4] = result.reshape(4, T, C)

    def sum_on(rel):
        step = 1 if rel > 0 else -1
        here = moe[POS[rel]]
        before = rel + step
        if before in POS and before != -8:
            arrived(rs_in.at[POS[rel]], ss_sem.at[POS[rel]], sr_sem.at[POS[rel]])
            here = here + rs_in[POS[rel]].astype(F32)
        rs_out[POS[rel]] = here.astype(BF16)
        slot = POS[rel - step] if rel - step else (0 if step > 0 else 16)
        send(rs_out.at[POS[rel]], rs_in.at[slot], ss_sem.at[POS[rel]], sr_sem.at[slot], plane(step))

    for n in (3, 2, 1, 0):
        combine(n)
        far = sorted(ORDER[4 * n : 4 * n + 4], key=lambda r: -abs(r))
        for rel in far:
            if rel:
                sum_on(rel)
    total = rows[0].astype(F32) + moe[0]
    for slot in (0, 16):
        arrived(rs_in.at[slot], ss_sem.at[1], sr_sem.at[slot])
        total = total + rs_in[slot].astype(F32)
    out_ref[...] = total.astype(BF16)

    for one in sends:
        one.wait_send()
    for core, one in special:

        @pl.when(c != core)
        def _(one=one):
            one.wait_send()


def body(
    hidden, draft_query, draft_kv, cache_kv, piece_offset, piece_length, ancestors, out_proj,
    ffn_gain, router_w, expert_gate_up, expert_down, expert_ids, accepted_ids,
):
    vmem = pl.BlockSpec(memory_space=pltpu.VMEM)
    smem = pl.BlockSpec(memory_space=pltpu.SMEM)
    hbm = pl.BlockSpec(memory_space=pl.ANY)
    dma = pltpu.SemaphoreType.DMA
    layer_out, attended, accepted = pl.pallas_call(
        kernel,
        out_shape=(
            jax.ShapeDtypeStruct((T, C), BF16),
            jax.ShapeDtypeStruct((T, C), BF16),
            jax.ShapeDtypeStruct((16, C), BF16),
        ),
        in_specs=[vmem, vmem, vmem, smem, smem, vmem, vmem, vmem, vmem, vmem, hbm, hbm, vmem, smem],
        out_specs=(vmem, vmem, vmem),
        scratch_shapes=[
            pltpu.VMEM((4, D, 256), BF16),
            pltpu.VMEM((512, D), BF16),
            pltpu.VMEM((4, T, C), BF16),
            pltpu.VMEM((7, T, C), BF16),
            pltpu.VMEM((4, T, 128), F32),
            pltpu.VMEM((4, T, C), BF16),
            pltpu.VMEM((4, T, 128), F32),
            pltpu.VMEM((4, T, C), F32),
            pltpu.VMEM((3, T, C), BF16),
            pltpu.VMEM((2, Z, 8, 128), F32),
            pltpu.VMEM((Z, 8, 128), F32),
            pltpu.VMEM((2, Z, 8, 128), F32),
            pltpu.VMEM((Z, 8, 128), F32),
            pltpu.VMEM((Z, T, C), BF16),
            pltpu.VMEM((4, T, C), BF16),
            pltpu.VMEM((4, 192, 256), BF16),
            pltpu.VMEM((4, 192, C), BF16),
            pltpu.VMEM((2, 192, D), BF16),
            pltpu.VMEM((192, D), BF16),
            pltpu.VMEM((192, 512), BF16),
            pltpu.VMEM((2, 192, D), BF16),
            pltpu.VMEM((4, 2, 192, C), BF16),
            pltpu.VMEM((Z, T, C), F32),
            pltpu.VMEM((Z, T, C), BF16),
            pltpu.VMEM((Z + 1, T, C), BF16),
            dma((3,)), dma((4, 3)), dma((4, 3)), dma((4,)), dma((4,)),
            dma((2, 4)), dma((2, 4)), dma((3,)), dma((3,)), dma((3,)), dma((3,)),
            dma((Z,)), dma((Z,)), dma((Z,)), dma((Z,)), dma((Z,)), dma((Z,)),
            dma((4, 8)), dma((2, 8, 2)), dma((2, 8, 2)), dma((4, 8)), dma((Z,)), dma((Z + 1,)),
        ],
        compiler_params=pltpu.CompilerParams(
            collective_id=0, has_side_effects=True, vmem_limit_bytes=56 * 2**20
        ),
        cost_estimate=pl.CostEstimate(flops=3 * 10**9, bytes_accessed=6 * 10**6, transcendentals=10**6),
        name="layer",
    )(
        draft_query, draft_kv, cache_kv, piece_offset, piece_length, ancestors, hidden, out_proj,
        ffn_gain.reshape(1, D), router_w, expert_gate_up, expert_down, expert_ids, accepted_ids,
    )
    return layer_out, attended, accepted.reshape(2, 8, C)


def solution(mesh):
    in_specs = (
        P("req", None),
        P("req", "tp"),
        P(None, "req", "tp"),
        P(None, "req", "tp"),
        P("req"),
        P("req"),
        P("req", None),
        P("tp", None),
        P(),
        P(),
        P(None, None, ("req", "tp")),
        P(("req", "tp"), None),
        P("req", None),
        P("req"),
    )
    out_specs = (P("req", "tp"), P("req", "tp"), P(None, "req", "tp"))
    return jax.shard_map(body, mesh=mesh, in_specs=in_specs, out_specs=out_specs, check_vma=False)
```
